256 devices in a mesh: section: 8 (over y, core), dp: 32 (over x, z).
Axes of the slice: x: 4, y: 4, z: 8, core: 2. Of those that a mesh axis runs over, the one named last changes fastest.
Arguments:
- hidden: bfloat16 [8192, 8192], P('dp'), may hold values from -100 to 100
- cluster: int32 [8192, 1], P('dp'), may hold values from 0 to 7; in each aligned block of 256 rows (0 to 255, 256 to 511, ...) at most 64 rows name the same one
- label: int32 [8192], P('dp'), may hold values from 0 to 16383
- proj: bfloat16 [8, 8192, 1024], P('section', 'dp'), may hold values from -0.0625 to 0.0625
- emb: bfloat16 [8, 1024, 16384], P('section', None, 'dp'), may hold values from -5 to 5
Outputs:
- loss: float32 [8192], P('dp')
The draws below stay inside these ranges and needn't reach their ends.
Inputs may be any that keep to these rules, and one draw needn't show every extreme that they name: The tokens of one index of dp name each cluster at most 64 times, a bound that some block reaches.
All inputs are finite; a program needn't handle non-finite values.
Results may differ from the reference program's by a relative error of at most 0.0003.
Values may be sent and summed in bfloat16 or wider, within the bound.
No kernel may reach another device: no remote copies, remote signals or barrier semaphores. Data moves between devices by JAX's collectives and lax.ppermute only.
A program may use at most 64 MiB of HBM per device.

```python
import math
import jax
import jax.numpy as jnp
import numpy as np
from jax import lax

D = 8192
R = 1024
VC = 16384
TOK_DEV = 256
CAP = 64
CLUSTERS = 8
TOKENS = 8192
N_DP = 32


def draw_hidden(key, part):
    key = jax.random.fold_in(key, 11)
    first, second, third = jax.random.split(key, 3)
    base = jnp.clip(jax.random.normal(first, (TOKENS, D), jnp.float32), -4.0, 4.0)
    lowest = 12.0
    highest = 24.0
    share = 32
    picked = jax.random.randint(second, (TOKENS, 1), 0, share) == 0
    sizes = jnp.exp(jax.random.uniform(third, (TOKENS, 1), jnp.float32, math.log(lowest), math.log(highest)))
    scales = jnp.where(picked, sizes, jnp.ones((TOKENS, 1), jnp.float32))
    return (base * scales).astype(jnp.bfloat16)


def draw_emb(key, part):
    key = jax.random.fold_in(key, 23)
    first = jax.random.fold_in(key, 0)
    third = jax.random.fold_in(key, 2)
    base = jnp.clip(jax.random.normal(first, (CLUSTERS, R, VC), jnp.float32), -4.0, 4.0) * (9.0 / R) ** 0.5
    column_scale = jnp.exp(jax.random.uniform(third, (CLUSTERS, 1, VC), jnp.float32, math.log(0.7), math.log(1.4)))
    return (base * column_scale).astype(jnp.bfloat16)


def touch_ends(drawn, own_key, least, high):
    dims = drawn.shape
    index_at = [jax.random.randint(jax.random.fold_in(own_key, axis), (), 0, dims[axis]) for axis in range(len(dims))]
    drawn = drawn.at[tuple(index_at)].set(least)
    longest = dims.index(max(dims))
    index_at[longest] = (index_at[longest] + 1) % dims[longest]
    return drawn.at[tuple(index_at)].set(high)


def levels(rng, shape, shards, least, largest):
    gain = 1.0
    for axis_at, blocks in shards:
        steps = jax.random.uniform(jax.random.fold_in(jax.random.fold_in(rng, 6), axis_at), (blocks,), jnp.float32, least / len(shards), largest / len(shards))
        gain = gain * jnp.repeat(jnp.exp(steps), shape[axis_at] // blocks).reshape((-1,) + (1,) * (len(shape) - 1 - axis_at))
    return gain


def deal_out(rng, own, number, rows, count, top, most, lean):
    ranking = jax.random.permutation(rng, count)
    crowded, usual = shares(count, rows * top, most, lean, True), shares(count, rows * top, most, lean, False)
    places = jnp.arange(count)

    def named(lengths, offset_by):
        used = int((lengths > 0).sum())
        fixed = max(1, used // 4)
        passed = fixed + (places - fixed + offset_by * (used - fixed)) % max(1, count - fixed)
        return jnp.zeros((count,), jnp.int32).at[ranking[jnp.where(places < fixed, places, passed)]].set(jnp.asarray(lengths, jnp.int32))

    lengths = jnp.where(number % 4 == 0, named(crowded, number // 4), named(usual, number - number // 4 - 1))
    mixed = jax.random.permutation(jax.random.fold_in(own, 3), count)
    source_of, receiver = mixed[0:count // 2 * 2:2], mixed[1:count // 2 * 2:2]
    slack = jnp.minimum(lengths[source_of] - 1, most - lengths[receiver]) // 2
    slack = jnp.where((source_of == ranking[0]) | (receiver == ranking[0]) | (lengths[receiver] == 0), 0, jnp.maximum(slack, 0))
    passed = jax.random.randint(jax.random.fold_in(own, 4), (count // 2,), 0, 1 << 20) % (slack + 1)
    lengths = lengths.at[source_of].add(-passed).at[receiver].add(passed)
    items = jnp.searchsorted(jnp.cumsum(lengths), jnp.arange(rows * top), side="right").astype(jnp.int32)
    table = items.reshape(top, rows).T
    table = table[jax.random.permutation(jax.random.fold_in(own, 1), rows)]
    offset_by = jax.random.randint(jax.random.fold_in(own, 2), (rows, 1), 0, top)
    return jnp.take_along_axis(table, (jnp.arange(top)[None, :] + offset_by) % top, axis=1)


def shares(count, total, reach, slope, full):
    portions = [(1 << 20) // math.isqrt(standing ** slope) + 1 for standing in range(1, count + 1)]
    largest = reach if full else min(reach, max(-(-total // count), total * portions[0] // sum(portions)))
    least = 1 if total - largest >= count - 1 else 0
    holding, spare = [largest] + [least] * (count - 1), total - largest - least * (count - 1)
    while spare > 0:
        candidates = [i for i in range(1, count) if holding[i] < largest] or [i for i in range(1, count) if holding[i] < reach]
        mass, remaining = sum([portions[i] for i in candidates]), spare
        for i in candidates:
            extra = min(reach - holding[i], max(1, remaining * portions[i] // mass), spare)
            holding[i] = holding[i] + extra
            spare = spare - extra
    return np.array(holding)


def gaussian(key, shape, deviation, reach, cuts=(), held_as=jnp.bfloat16):
    array = jax.random.normal(key, shape, jnp.float32) * deviation
    if len(cuts) > 0:
        array = levels(key, shape, cuts, -0.22, 0.18) * array
    return jnp.clip(array, min=-reach, max=reach).astype(held_as)


def setup_inputs(seed: int = 0) -> dict:
    key_of = jax.random.split(jax.random.key(seed), 6)
    hidden = draw_hidden(jax.random.fold_in(key_of[5], 71), 0)
    cluster_keys = jax.random.split(jax.random.fold_in(key_of[1], 1), TOKENS // TOK_DEV)
    cluster_turns = jax.random.permutation(jax.random.fold_in(key_of[1], 3), TOKENS // TOK_DEV)
    cluster = jax.vmap(lambda own, number: deal_out(jax.random.fold_in(key_of[1], 2), own, number, TOK_DEV, CLUSTERS, 1, CAP, 2))(cluster_keys, cluster_turns).reshape((TOKENS, 1))
    label = touch_ends(jax.random.randint(key_of[2], (TOKENS,), 0, VC), jax.random.fold_in(key_of[2], 1), 0, VC - 1).astype(jnp.int32)
    proj = gaussian(key_of[3], (CLUSTERS, D, R), D ** -0.5, 0.0625, ((0, 8), (1, 32)))
    emb = draw_emb(jax.random.fold_in(key_of[5], 71), 0)
    return dict(hidden=hidden, cluster=cluster, label=label, proj=proj, emb=emb)


def reference(hidden, cluster, label, proj, emb):
    ids = cluster[:, 0]
    tokens = hidden.shape[0]
    slots_all = CAP * N_DP
    order = jnp.arange(tokens, dtype=jnp.int32)
    block = order // TOK_DEV

    def one_cluster(index):
        mine = ids == index
        within = jnp.cumsum(mine.astype(jnp.int32).reshape(N_DP, TOK_DEV), axis=1).reshape(tokens) - 1
        target = jnp.where(mine, block * CAP + within, slots_all).astype(jnp.int32)
        picks = jnp.zeros((slots_all,), jnp.int32).at[target].set(order, mode="drop")
        rows = hidden[picks]
        weight = lax.dynamic_index_in_dim(proj, index, 0, keepdims=False)
        table = lax.dynamic_index_in_dim(emb, index, 0, keepdims=False)
        projected = jnp.dot(rows, weight, preferred_element_type=jnp.float32)
        logits = jnp.dot(projected, table.astype(jnp.float32), precision=lax.Precision.HIGHEST, preferred_element_type=jnp.float32)
        top = jnp.max(logits, axis=1)
        lse = top + jnp.log(jnp.sum(jnp.exp(logits - top[:, None]), axis=1))
        words = label[picks]
        chosen = jnp.take_along_axis(logits, words[:, None], axis=1)[:, 0]
        slot_loss = lse - chosen
        safe = jnp.minimum(target, slots_all - 1).astype(jnp.int32)
        return jnp.where(mine, slot_loss[safe], jnp.zeros((), jnp.float32))

    parts = lax.map(one_cluster, jnp.arange(CLUSTERS, dtype=jnp.int32))
    return jnp.sum(parts, axis=0)
```

```python
import jax
import jax.numpy as jnp
from jax import lax
from jax.experimental import pallas as pl
from jax.experimental.pallas import tpu as pltpu
from jax.sharding import Mesh
from jax.sharding import PartitionSpec as P

CAP = 64
X = 4
Z = 8
BF16 = jnp.bfloat16
F16 = jnp.float16
F32 = jnp.float32
VMEM_LIMIT = 40 * 1024 * 1024


def ring(array, axis, size, step):
    return lax.ppermute(array, axis, [(i, (i + step) % size) for i in range(size)])


def params():
    return pltpu.CompilerParams(vmem_limit_bytes=VMEM_LIMIT)


def cost(flops, moved):
    return pl.CostEstimate(flops=flops, bytes_accessed=moved, transcendentals=0)


def slot_choice(ids, owner):
    tokens = ids.shape[1]
    mine = ids == owner
    ones = jnp.where(mine, 1.0, 0.0).astype(F32)
    earlier = lax.broadcasted_iota(jnp.int32, (tokens, tokens), 0)
    later = lax.broadcasted_iota(jnp.int32, (tokens, tokens), 1)
    upto = jnp.where(earlier <= later, 1.0, 0.0).astype(F32)
    within = jnp.dot(
        jnp.broadcast_to(ones, (8, tokens)), upto, preferred_element_type=F32
    )[0:1, :]
    place = lax.broadcasted_iota(jnp.int32, (CAP, tokens), 0)
    within = (within + 0.5).astype(jnp.int32) - 1
    return (within == place) & mine


def select_kernel(where_ref, ids_ref, label_ref, hidden_ref, *outs):
    pieces, words_ref, choice_ref = outs[:X], outs[X], outs[X + 1]
    owner, z = where_ref[0], where_ref[2]
    step = pl.program_id(0)

    @pl.when(step == 0)
    def _():
        choice = slot_choice(ids_ref[...], owner)
        choice_ref[...] = jnp.where(choice, 1.0, 0.0).astype(BF16)
        word = jnp.sum(jnp.where(choice, label_ref[...], 0), axis=1, keepdims=True)
        lane = lax.broadcasted_iota(jnp.int32, (CAP, 128), 1)
        parts = jnp.where(lane == 0, word >> 7, jnp.where(lane == 1, word & 127, 0))
        words_ref[...] = parts.astype(F32)

    depth = hidden_ref.shape[1] // Z
    for k in range(X):

        @pl.when(step == k)
        def _(k=k):
            for j in range(Z):
                at = pl.multiple_of(lax.rem(z + j, Z) * depth, depth)
                rows = jnp.dot(
                    choice_ref[...],
                    hidden_ref[:, pl.ds(at, depth)],
                    preferred_element_type=F32,
                )
                pieces[k][:, j * depth : (j + 1) * depth] = rows.astype(BF16)


def select_rows(where, ids, label, hidden):
    tokens, width = hidden.shape
    part = width // X
    whole = lambda shape: pl.BlockSpec(shape, lambda k, w: (0, 0))
    return pl.pallas_call(
        select_kernel,
        grid_spec=pltpu.PrefetchScalarGridSpec(
            num_scalar_prefetch=1,
            grid=(X,),
            in_specs=[
                whole((1, tokens)),
                whole((1, tokens)),
                pl.BlockSpec((tokens, part), lambda k, w: (0, lax.rem(w[1] + k, X))),
            ],
            out_specs=[whole((CAP, part))] * X + [whole((CAP, 128))],
            scratch_shapes=[pltpu.VMEM((CAP, tokens), BF16)],
        ),
        out_shape=[jax.ShapeDtypeStruct((CAP, part), BF16)] * X
        + [jax.ShapeDtypeStruct((CAP, 128), F32)],
        compiler_params=params(),
        cost_estimate=cost(2 * CAP * tokens * width, 2 * tokens * width),
    )(where, ids, label, hidden)


def project_first_kernel(offsets, *refs):
    rows, chunks, out = refs[:X], refs[X : X + len(offsets)], refs[-1]
    depth = chunks[0].shape[0]
    left = jnp.concatenate([r[...] for r in rows], axis=0)
    total = None
    for offset, chunk in zip(offsets, chunks):
        term = jnp.dot(
            left[:, offset * depth : (offset + 1) * depth],
            chunk[...],
            preferred_element_type=F32,
        )
        total = term if total is None else total + term
    out[...] = total


def project_first(rows, chunks, offsets):
    depth, wide = chunks[0].shape
    return pl.pallas_call(
        lambda *refs: project_first_kernel(offsets, *refs),
        out_shape=jax.ShapeDtypeStruct((X * CAP, wide), F32),
        compiler_params=params(),
        cost_estimate=cost(2 * X * CAP * depth * len(chunks) * wide, 6_000_000),
    )(*rows, *chunks)


def project_last_kernel(total_ref, *refs):
    rows, front, back, outs = refs[:X], refs[X], refs[X + 1], refs[X + 2 :]
    half = front.shape[0]
    left = jnp.concatenate([r[...] for r in rows], axis=0)
    total = total_ref[...]
    total += jnp.dot(left[:, :half], front[...], preferred_element_type=F32)
    total += jnp.dot(left[:, half:], back[...], preferred_element_type=F32)
    for k in range(X):
        outs[k][...] = total[k * CAP : (k + 1) * CAP, :].astype(outs[k].dtype)


def project_last(total, rows, front, back, held):
    half, wide = front.shape
    depth = 2 * half
    at = lambda *index: lambda i: index
    return pl.pallas_call(
        project_last_kernel,
        grid=(1,),
        in_specs=[pl.BlockSpec(total.shape, at(0, 0))]
        + [pl.BlockSpec((CAP, depth), at(0, Z // 2))] * X
        + [pl.BlockSpec((half, wide), at(0, 0))] * 2,
        out_specs=[pl.BlockSpec((CAP, wide), at(0, 0))] * X,
        out_shape=[jax.ShapeDtypeStruct((CAP, wide), held)] * X,
        compiler_params=params(),
        cost_estimate=cost(2 * X * CAP * depth * wide, 3_000_000),
    )(total, *rows, front, back)


def word_kernel(last, blocks, where_ref, high_ref, low_ref, word_ref, emb_ref, *refs):
    before = refs[0] if last else None
    out_ref, top_ref, sum_ref, hit_ref = refs[1:] if last else refs
    z = where_ref[2]
    part = pl.program_id(0)
    width = emb_ref.shape[2]

    @pl.when(part == 0)
    def _():
        top_ref[...] = jnp.full(top_ref.shape, -jnp.inf, F32)
        sum_ref[...] = jnp.zeros(sum_ref.shape, F32)
        hit_ref[...] = jnp.zeros(hit_ref.shape, F32)

    table = emb_ref[0]
    logits = jnp.dot(high_ref[...], table, preferred_element_type=F32)
    logits += jnp.dot(low_ref[...], table, preferred_element_type=F32)
    codes = word_ref[...]
    word = (codes[:, 0:1] * 128.0 + codes[:, 1:2]).astype(jnp.int32)
    local = word - (part * Z + z) * width
    column = lax.broadcasted_iota(jnp.int32, (logits.shape[0], 128), 1)
    tiles = [logits[:, i * 128 : (i + 1) * 128] for i in range(width // 128)]
    top = top_ref[...]
    best = top
    for tile in tiles:
        best = jnp.maximum(best, tile)
    total = sum_ref[...] * jnp.exp(top - best)
    hit = hit_ref[...]
    for i, tile in enumerate(tiles):
        total += jnp.exp(tile - best)
        hit += jnp.where(column + i * 128 == local, tile, 0.0)
    top_ref[...] = best
    sum_ref[...] = total
    hit_ref[...] = hit

    @pl.when(part == X - 1)
    def _():
        highest = jnp.max(best, axis=1, keepdims=True)
        summed = jnp.sum(total * jnp.exp(best - highest), axis=1, keepdims=True)
        chosen = jnp.sum(hit, axis=1, keepdims=True)
        stats = jnp.where(
            column == 0,
            highest,
            jnp.where(column == 1, summed, jnp.where(column == 2, chosen, 0.0)),
        )
        for i, back in enumerate(blocks):
            rows = stats[i * CAP : (i + 1) * CAP, :]
            turned = jnp.concatenate([rows, rows], axis=0).T[0:8, :]
            if last:
                out_ref[lax.rem(z - back + Z, Z)] = turned
            else:
                out_ref[i] = turned
        if last:
            done = refs[0].shape[0]
            for i, back in enumerate(FIRST[:done]):
                out_ref[lax.rem(z - back + Z, Z)] = before[i]


FIRST = (0, 1, 7, 2, 6)
SECOND = (3, 5, 4)


def word_stats(where, high, low, words, emb, before=None):
    last = before is not None
    blocks = SECOND if last else FIRST
    rows, depth = high.shape
    width = emb.shape[2]
    whole = lambda shape: pl.BlockSpec(shape, lambda k, w: (0,) * len(shape))
    count = Z if last else len(blocks)
    return pl.pallas_call(
        lambda *refs: word_kernel(last, blocks, *refs),
        grid_spec=pltpu.PrefetchScalarGridSpec(
            num_scalar_prefetch=1,
            grid=(X,),
            in_specs=[
                whole((rows, depth)),
                whole((rows, depth)),
                whole((rows, 128)),
                pl.BlockSpec((1, depth, width), lambda k, w: (k, 0, 0)),
            ]
            + ([whole(before.shape)] if last else []),
            out_specs=whole((count, 8, 128)),
            scratch_shapes=[pltpu.VMEM((rows, 128), F32)] * 3,
        ),
        out_shape=jax.ShapeDtypeStruct((count, 8, 128), F32),
        compiler_params=params(),
        cost_estimate=cost(4 * rows * depth * width * X, 2 * depth * width * X),
    )(where, high, low, words, emb, *((before,) if last else ()))


def combine_kernel(where_ref, ids_ref, stats_ref, out_ref):
    stats = stats_ref[...]
    top, total, chosen = stats[:, 0, :], stats[:, 1, :], stats[:, 2, :]
    highest = jnp.max(top, axis=0, keepdims=True)
    summed = jnp.sum(total * jnp.exp(top - highest), axis=0, keepdims=True)
    loss = highest + jnp.log(summed) - jnp.sum(chosen, axis=0, keepdims=True)
    column = jnp.broadcast_to(loss, (128, 128)).T[0:CAP, 0:1]
    choice = slot_choice(ids_ref[...], where_ref[0])
    out_ref[...] = jnp.sum(jnp.where(choice, column, 0.0), axis=0, keepdims=True)


def combine(where, ids, stats):
    tokens = ids.shape[1]
    return pl.pallas_call(
        combine_kernel,
        in_specs=[
            pl.BlockSpec(memory_space=pltpu.SMEM),
            pl.BlockSpec(memory_space=pltpu.VMEM),
            pl.BlockSpec(memory_space=pltpu.VMEM),
        ],
        out_shape=jax.ShapeDtypeStruct((1, tokens), F32),
        compiler_params=params(),
        cost_estimate=cost(2 * 8 * tokens * tokens, 50_000),
    )(where, ids, stats)


def split(blocks, width):
    held = jnp.concatenate(blocks, axis=0)
    wide = held[:, :width].astype(F32)
    high = lax.reduce_precision(wide, exponent_bits=8, mantissa_bits=7)
    return high.astype(BF16), (wide - high).astype(BF16), held[:, width:].astype(F32)


def body(hidden, cluster, label, proj, emb):
    x, z = lax.axis_index("x"), lax.axis_index("z")
    owner = lax.axis_index("y") * 2 + lax.axis_index("core")
    where = jnp.stack([owner, x, z]).astype(jnp.int32)
    ids = cluster.reshape(1, -1)
    weight = proj[0]
    half = weight.shape[0] // 2
    wide = weight.shape[1]

    table = lax.all_gather(emb[0], "x", axis=0)

    *pieces, words = select_rows(where, ids, label.reshape(1, -1), hidden)
    rows = [pieces[0]] + [ring(pieces[k], "x", X, k) for k in range(1, X)]

    chunks, offsets = [weight], [0]
    right = left = weight
    for s in range(1, Z // 2):
        right, left = ring(right, "z", Z, 1), ring(left, "z", Z, -1)
        chunks += [right, left]
        offsets += [Z - s, s]
    front = ring(right[:half], "z", Z, 1)
    back = ring(left[half:], "z", Z, -1)

    total = project_first(rows, chunks, offsets)
    parts = project_last(total, rows, front, back, F32)
    own = parts[0]
    for k in range(1, X):
        own = own + ring(parts[k], "x", X, -k)

    message = jnp.concatenate([own, words], axis=1).astype(F16)
    r1, l1 = ring(message, "z", Z, 1), ring(message, "z", Z, -1)
    r2, l2 = ring(message, "z", Z, 2), ring(message, "z", Z, -2)
    r3, l3 = ring(r2, "z", Z, 1), ring(l2, "z", Z, -1)
    r4 = ring(r2, "z", Z, 2)

    stats = word_stats(where, *split([message, r1, l1, r2, l2], wide), table)
    stats = word_stats(where, *split([r3, l3, r4], wide), table, stats)
    stats = lax.all_to_all(stats, "z", 0, 0, tiled=True)
    loss = combine(where, ids, stats)
    loss = loss + lax.ppermute(loss, "core", [(0, 1), (1, 0)])
    loss = loss + ring(loss, "y", 4, 1) + ring(loss, "y", 4, 2) + ring(loss, "y", 4, 3)
    return loss.reshape(-1)


def solution(mesh):
    fine = Mesh(mesh.devices.reshape(4, 2, X, Z), ("y", "core", "x", "z"))
    return jax.shard_map(
        body,
        mesh=fine,
        in_specs=(
            P(("x", "z"), None),
            P(("x", "z"), None),
            P(("x", "z")),
            P(("y", "core"), ("x", "z"), None),
            P(("y", "core"), None, ("x", "z")),
        ),
        out_specs=P(("x", "z")),
        check_vma=False,
    )
```

```python
import jax
import jax.numpy as jnp
from jax import lax
from jax.experimental import pallas as pl
from jax.experimental.pallas import tpu as pltpu
from jax.sharding import Mesh
from jax.sharding import PartitionSpec as P

CAP = 64
X = 4
Z = 8
SECTIONS = 8
BF16 = jnp.bfloat16
F16 = jnp.float16
F32 = jnp.float32
VMEM_LIMIT = 40 * 1024 * 1024


def ring(array, axis, size, step):
    return lax.ppermute(array, axis, [(i, (i + step) % size) for i in range(size)])


def params():
    return pltpu.CompilerParams(vmem_limit_bytes=VMEM_LIMIT)


def cost(flops, moved):
    return pl.CostEstimate(flops=flops, bytes_accessed=moved, transcendentals=0)


def slot_choice(ids, owner):
    tokens = ids.shape[1]
    mine = ids == owner
    ones = jnp.where(mine, 1.0, 0.0).astype(F32)
    earlier = lax.broadcasted_iota(jnp.int32, (tokens, tokens), 0)
    later = lax.broadcasted_iota(jnp.int32, (tokens, tokens), 1)
    upto = jnp.where(earlier <= later, 1.0, 0.0).astype(F32)
    within = jnp.dot(
        jnp.broadcast_to(ones, (8, tokens)), upto, preferred_element_type=F32
    )[0:1, :]
    place = lax.broadcasted_iota(jnp.int32, (CAP, tokens), 0)
    within = (within + 0.5).astype(jnp.int32) - 1
    return (within == place) & mine


def select_kernel(
    where_ref, ids_ref, label_ref, hidden_ref, own_ref, up_ref, down_ref, words_ref, choice_ref
):
    owner, z = where_ref[0], where_ref[2]
    step = pl.program_id(0)

    @pl.when(step == 0)
    def _():
        choice = slot_choice(ids_ref[...], owner)
        choice_ref[...] = jnp.where(choice, 1.0, 0.0).astype(BF16)
        word = jnp.sum(jnp.where(choice, label_ref[...], 0), axis=1, keepdims=True)
        lane = lax.broadcasted_iota(jnp.int32, (CAP, 128), 1)
        parts = jnp.where(lane == 0, word >> 7, jnp.where(lane == 1, word & 127, 0))
        words_ref[...] = parts.astype(F32)

    part = hidden_ref.shape[1]
    depth, half = part // Z, part // 2

    def pick(j):
        at = pl.multiple_of(lax.rem(z + j, Z) * depth, depth)
        rows = jnp.dot(
            choice_ref[...], hidden_ref[:, pl.ds(at, depth)], preferred_element_type=F32
        )
        return rows.astype(BF16)

    for k, target in enumerate((own_ref, up_ref, None, down_ref)):

        @pl.when(step == k)
        def _(target=target):
            for j in range(Z):
                at = j * depth
                if target is not None:
                    target[:, at : at + depth] = pick(j)
                elif at < half:
                    up_ref[:, part + at : part + at + depth] = pick(j)
                else:
                    down_ref[:, half + at : half + at + depth] = pick(j)


def select_rows(where, ids, label, hidden):
    tokens, width = hidden.shape
    part = width // X
    whole = lambda shape: pl.BlockSpec(shape, lambda k, w: (0, 0))
    shapes = [(CAP, part), (CAP, part * 3 // 2), (CAP, part * 3 // 2)]
    return pl.pallas_call(
        select_kernel,
        grid_spec=pltpu.PrefetchScalarGridSpec(
            num_scalar_prefetch=1,
            grid=(X,),
            in_specs=[
                whole((1, tokens)),
                whole((1, tokens)),
                pl.BlockSpec((tokens, part), lambda k, w: (0, lax.rem(w[1] + k, X))),
            ],
            out_specs=[whole(shape) for shape in shapes] + [whole((CAP, 128))],
            scratch_shapes=[pltpu.VMEM((CAP, tokens), BF16)],
        ),
        out_shape=[jax.ShapeDtypeStruct(shape, BF16) for shape in shapes]
        + [jax.ShapeDtypeStruct((CAP, 128), F32)],
        compiler_params=params(),
        cost_estimate=cost(2 * CAP * tokens * width, 2 * tokens * width),
    )(where, ids, label, hidden)


def project_first_kernel(offsets, *refs):
    rows, chunks, out = refs[:X], refs[X : X + len(offsets)], refs[-1]
    depth = chunks[0].shape[0]
    part = depth * Z
    left = jnp.concatenate([r[:, :part] for r in rows], axis=0)
    total = None
    for offset, chunk in zip(offsets, chunks):
        term = jnp.dot(
            left[:, offset * depth : (offset + 1) * depth],
            chunk[...],
            preferred_element_type=F32,
        )
        total = term if total is None else total + term
    out[...] = total


def project_first(rows, chunks, offsets):
    depth, wide = chunks[0].shape
    return pl.pallas_call(
        lambda *refs: project_first_kernel(offsets, *refs),
        out_shape=jax.ShapeDtypeStruct((X * CAP, wide), F32),
        compiler_params=params(),
        cost_estimate=cost(2 * X * CAP * depth * len(chunks) * wide, 6_000_000),
    )(*rows, *chunks)


def project_last_kernel(total_ref, *refs):
    rows, front, back, outs = refs[:X], refs[X], refs[X + 1], refs[X + 2 :]
    half = front.shape[0]
    left = jnp.concatenate([r[...] for r in rows], axis=0)
    total = total_ref[...]
    total += jnp.dot(left[:, :half], front[...], preferred_element_type=F32)
    total += jnp.dot(left[:, half:], back[...], preferred_element_type=F32)
    for k in range(X):
        outs[k][...] = total[k * CAP : (k + 1) * CAP, :].astype(outs[k].dtype)


def project_last(total, rows, front, back, held):
    half, wide = front.shape
    depth = 2 * half
    at = lambda *index: lambda i: index
    return pl.pallas_call(
        project_last_kernel,
        grid=(1,),
        in_specs=[pl.BlockSpec(total.shape, at(0, 0))]
        + [pl.BlockSpec((CAP, depth), at(0, Z // 2))] * X
        + [pl.BlockSpec((half, wide), at(0, 0))] * 2,
        out_specs=[pl.BlockSpec((CAP, wide), at(0, 0))] * X,
        out_shape=[jax.ShapeDtypeStruct((CAP, wide), held)] * X,
        compiler_params=params(),
        cost_estimate=cost(2 * X * CAP * depth * wide, 3_000_000),
    )(total, *rows, front, back)


FIRST = (0, 1, 7, 2, 6)
SECOND = (3, 5, 4)


def word_kernel(last, blocks, where_ref, both_ref, word_ref, *refs):
    tables, refs = refs[: X + 1], refs[X + 1 :]
    before = refs[0] if last else None
    out_ref, held, arrived = refs[1:] if last else refs
    x, z = where_ref[1], where_ref[2]
    rows = word_ref.shape[0]
    width = held.shape[2]
    half = held.shape[1] // 2
    spots = [
        held.at[0],
        held.at[1],
        held.at[2],
        held.at[3, pl.ds(0, half)],
        held.at[3, pl.ds(half, half)],
    ]
    copies = [
        pltpu.make_async_copy(
            table.at[pl.ds(0, spot.shape[0])], spot, arrived.at[i]
        )
        for i, (table, spot) in enumerate(zip(tables, spots))
    ]
    for copy in copies:
        copy.start()

    codes = word_ref[...]
    word = (codes[:, 0:1] * 128.0 + codes[:, 1:2]).astype(jnp.int32)
    column = lax.broadcasted_iota(jnp.int32, (rows, 128), 1)
    best = total = hit = None
    for part, back in enumerate((0, 1, 3, 2)):
        copies[part].wait()
        if part == X - 1:
            copies[X].wait()
        products = jnp.dot(both_ref[...], held[part], preferred_element_type=F32)
        logits = products[:rows] + products[rows:]
        local = word - (lax.rem(x - back + X, X) * Z + z) * width
        tiles = [logits[:, i * 128 : (i + 1) * 128] for i in range(width // 128)]
        peak = tiles[0]
        for tile in tiles[1:]:
            peak = jnp.maximum(peak, tile)
        if best is None:
            best, total, hit = peak, jnp.zeros_like(peak), jnp.zeros_like(peak)
        else:
            peak = jnp.maximum(best, peak)
            best, total = peak, total * jnp.exp(best - peak)
        for i, tile in enumerate(tiles):
            total += jnp.exp(tile - best)
            hit += jnp.where(column + i * 128 == local, tile, 0.0)

    highest = jnp.max(best, axis=1, keepdims=True)
    summed = jnp.sum(total * jnp.exp(best - highest), axis=1, keepdims=True)
    chosen = jnp.sum(hit, axis=1, keepdims=True)
    stats = jnp.where(
        column == 0,
        highest,
        jnp.where(column == 1, summed, jnp.where(column == 2, chosen, 0.0)),
    )
    for i, back in enumerate(blocks):
        piece = stats[i * CAP : (i + 1) * CAP, :]
        turned = jnp.concatenate([piece, piece], axis=0).T
        top_sum = jnp.where(column[0:1] < CAP, turned[0:1], turned[1:2])
        pair = jnp.concatenate([top_sum, turned[2:3]], axis=0)
        if last:
            for s in range(SECTIONS):
                out_ref[s, lax.rem(z - back + Z, Z)] = pair
        else:
            out_ref[i] = pair
    if last:
        for i, back in enumerate(FIRST):
            for s in range(SECTIONS):
                out_ref[s, lax.rem(z - back + Z, Z)] = before[i]


def word_stats(where, both, words, tables, before=None):
    last = before is not None
    blocks = SECOND if last else FIRST
    rows, depth = words.shape[0], both.shape[1]
    width = tables[0].shape[1]
    inside = pl.BlockSpec(memory_space=pltpu.VMEM)
    return pl.pallas_call(
        lambda *refs: word_kernel(last, blocks, *refs),
        in_specs=[pl.BlockSpec(memory_space=pltpu.SMEM), inside, inside]
        + [pl.BlockSpec(memory_space=pl.ANY)] * (X + 1)
        + ([inside] if last else []),
        out_specs=inside,
        out_shape=jax.ShapeDtypeStruct(
            ((SECTIONS, Z) if last else (len(blocks),)) + (2, 128), F32
        ),
        scratch_shapes=[
            pltpu.VMEM((X, depth, width), BF16),
            pltpu.SemaphoreType.DMA((X + 1,)),
        ],
        compiler_params=params(),
        cost_estimate=cost(4 * rows * depth * width * X, 2 * depth * width * X),
    )(where, both, words, *tables, *((before,) if last else ()))


def combine_kernel(ids_ref, stats_ref, out_ref):
    stats = stats_ref[...]
    tokens = ids_ref.shape[1]
    top, total, chosen = stats[:, :, 0, :CAP], stats[:, :, 0, CAP:], stats[:, :, 1, :CAP]
    highest = jnp.max(top, axis=1, keepdims=True)
    summed = jnp.sum(total * jnp.exp(top - highest), axis=1)
    loss = highest[:, 0] + jnp.log(summed) - jnp.sum(chosen, axis=1)
    columns = jnp.concatenate(
        [
            jnp.concatenate([loss, jnp.zeros((SECTIONS, 128 - CAP), F32)], axis=1),
            jnp.zeros((128 - SECTIONS, 128), F32),
        ],
        axis=0,
    ).T
    ids = ids_ref[...]
    owner = lax.broadcasted_iota(jnp.int32, (SECTIONS, tokens), 0)
    mine = jnp.where(ids == owner, 1.0, 0.0).astype(F32)
    earlier = lax.broadcasted_iota(jnp.int32, (tokens, tokens), 0)
    later = lax.broadcasted_iota(jnp.int32, (tokens, tokens), 1)
    upto = jnp.where(earlier <= later, 1.0, 0.0).astype(F32)
    within = jnp.dot(mine, upto, preferred_element_type=F32)
    slot = jnp.sum(within * mine, axis=0, keepdims=True)
    slot = (slot + 0.5).astype(jnp.int32) - 1
    place = lax.broadcasted_iota(jnp.int32, (CAP, tokens), 0)
    found = jnp.zeros((CAP, tokens), F32)
    for s in range(SECTIONS):
        found = jnp.where(ids == s, columns[0:CAP, s : s + 1], found)
    out_ref[...] = jnp.sum(jnp.where(place == slot, found, 0.0), axis=0, keepdims=True)


def combine(ids, stats):
    tokens = ids.shape[1]
    return pl.pallas_call(
        combine_kernel,
        out_shape=jax.ShapeDtypeStruct((1, tokens), F32),
        compiler_params=params(),
        cost_estimate=cost(2 * 8 * tokens * tokens, 400_000),
    )(ids, stats)


def split(blocks, width):
    held = jnp.concatenate(blocks, axis=0)
    wide = held[:, :width].astype(F32)
    high = lax.reduce_precision(wide, exponent_bits=8, mantissa_bits=7)
    both = jnp.concatenate([high, wide - high], axis=0).astype(BF16)
    return both, held[:, width:].astype(F32)


def relay(table, message, part):
    width = table.shape[1]
    return jnp.concatenate(
        [table, message[:, part : part + width], message[:, part + width :]], axis=0
    )


def body(hidden, cluster, label, proj, emb):
    x, z = lax.axis_index("x"), lax.axis_index("z")
    owner = lax.axis_index("y") * 2 + lax.axis_index("core")
    where = jnp.stack([owner, x, z]).astype(jnp.int32)
    ids = cluster.reshape(1, -1)
    weight, table = proj[0], emb[0]
    half = weight.shape[0] // 2
    wide = weight.shape[1]
    middle = table.shape[0] // 2

    deep = table.shape[0]
    right1, left1 = ring(weight, "z", Z, 1), ring(weight, "z", Z, -1)
    own_rows, up, down, words = select_rows(where, ids, label.reshape(1, -1), hidden)
    part = own_rows.shape[1]
    up, down = ring(up, "x", X, 1), ring(down, "x", X, -1)
    right1, left1, words = lax.optimization_barrier((right1, left1, words))
    right2, left2 = ring(right1, "z", Z, 1), ring(left1, "z", Z, -1)
    up, down, _, _ = lax.optimization_barrier((up, down, right1, left1))
    after = ring(relay(table, up, part), "x", X, 1)
    ahead = ring(relay(table, down, part), "x", X, -1)
    right3, left3 = ring(right2, "z", Z, 1), ring(left2, "z", Z, -1)
    front = ring(right3[:half], "z", Z, 1)
    back = ring(left3[half:], "z", Z, -1)
    front, back, after, ahead = lax.optimization_barrier((front, back, after, ahead))
    far1 = ring(after[:middle], "x", X, 1)
    far2 = ring(ahead[middle:deep], "x", X, -1)
    tables = [table, after, ahead, far1, far2]
    across = jnp.concatenate(
        [side[deep + i : deep + i + CAP] for side in (after, ahead) for i in (0, CAP)],
        axis=1,
    )
    rows = [own_rows, up, across, down]

    chunks = [weight, right1, left1, right2, left2, right3, left3]
    total = project_first(rows, chunks, [0, 7, 1, 6, 2, 5, 3])
    parts = project_last(total, rows, front, back, F32)
    own = parts[0]
    for k in range(1, X):
        own = own + ring(parts[k].astype(F16), "x", X, -k).astype(F32)

    message = jnp.concatenate([own, words], axis=1).astype(F16)
    r1, l1 = ring(message, "z", Z, 1), ring(message, "z", Z, -1)
    r2, l2 = ring(message, "z", Z, 2), ring(message, "z", Z, -2)
    r3, l3 = ring(r2, "z", Z, 1), ring(l2, "z", Z, -1)
    r4 = ring(r2, "z", Z, 2)

    stats = word_stats(where, *split([message, r1, l1, r2, l2], wide), tables)
    stats, r3, l3, r4 = lax.optimization_barrier((stats, r3, l3, r4))
    stats = word_stats(where, *split([r3, l3, r4], wide), tables, stats)
    stats = stats.reshape(SECTIONS * Z, 2, 128)
    stats = lax.all_to_all(stats, ("y", "core", "z"), 0, 0, tiled=True)
    loss = combine(ids, stats.reshape(SECTIONS, Z, 2, 128))
    return loss.reshape(-1)


def solution(mesh):
    fine = Mesh(mesh.devices.reshape(4, 2, X, Z), ("y", "core", "x", "z"))
    return jax.shard_map(
        body,
        mesh=fine,
        in_specs=(
            P(("x", "z"), None),
            P(("x", "z"), None),
            P(("x", "z")),
            P(("y", "core"), ("x", "z"), None),
            P(("y", "core"), None, ("x", "z")),
        ),
        out_specs=P(("x", "z")),
        check_vma=False,
    )
```

```python
import jax
import jax.numpy as jnp
from jax import lax
from jax.experimental import pallas as pl
from jax.experimental.pallas import tpu as pltpu
from jax.sharding import Mesh
from jax.sharding import PartitionSpec as P

CAP = 64
X = 4
Z = 8
SECTIONS = 8
BF16 = jnp.bfloat16
F16 = jnp.float16
F32 = jnp.float32
VMEM_LIMIT = 40 * 1024 * 1024


def ring(array, axis, size, step):
    return lax.ppermute(array, axis, [(i, (i + step) % size) for i in range(size)])


def params():
    return pltpu.CompilerParams(vmem_limit_bytes=VMEM_LIMIT)


def cost(flops, moved):
    return pl.CostEstimate(flops=flops, bytes_accessed=moved, transcendentals=0)


def slot_choice(ids, owner):
    tokens = ids.shape[1]
    mine = ids == owner
    ones = jnp.where(mine, 1.0, 0.0).astype(F32)
    earlier = lax.broadcasted_iota(jnp.int32, (tokens, tokens), 0)
    later = lax.broadcasted_iota(jnp.int32, (tokens, tokens), 1)
    upto = jnp.where(earlier <= later, 1.0, 0.0).astype(F32)
    within = jnp.dot(
        jnp.broadcast_to(ones, (8, tokens)), upto, preferred_element_type=F32
    )[0:1, :]
    place = lax.broadcasted_iota(jnp.int32, (CAP, tokens), 0)
    within = (within + 0.5).astype(jnp.int32) - 1
    return (within == place) & mine


def select_kernel(
    where_ref, ids_ref, label_ref, hidden_ref, own_ref, up_ref, down_ref, words_ref, choice_ref
):
    owner, z = where_ref[0], where_ref[2]
    step = pl.program_id(0)

    @pl.when(step == 0)
    def _():
        choice = slot_choice(ids_ref[...], owner)
        choice_ref[...] = jnp.where(choice, 1.0, 0.0).astype(BF16)
        word = jnp.sum(jnp.where(choice, label_ref[...], 0), axis=1, keepdims=True)
        lane = lax.broadcasted_iota(jnp.int32, (CAP, 128), 1)
        parts = jnp.where(lane == 0, word >> 7, jnp.where(lane == 1, word & 127, 0))
        words_ref[...] = parts.astype(F32)

    part = hidden_ref.shape[1]
    depth, half = part // Z, part // 2

    def pick(j):
        at = pl.multiple_of(lax.rem(z + j, Z) * depth, depth)
        rows = jnp.dot(
            choice_ref[...], hidden_ref[:, pl.ds(at, depth)], preferred_element_type=F32
        )
        return rows.astype(BF16)

    for k, target in enumerate((own_ref, up_ref, None, down_ref)):

        @pl.when(step == k)
        def _(target=target):
            for j in range(Z):
                at = j * depth
                if target is not None:
                    target[:, at : at + depth] = pick(j)
                elif at < half:
                    up_ref[:, part + at : part + at + depth] = pick(j)
                else:
                    down_ref[:, half + at : half + at + depth] = pick(j)


def select_rows(where, ids, label, hidden):
    tokens, width = hidden.shape
    part = width // X
    whole = lambda shape: pl.BlockSpec(shape, lambda k, w: (0, 0))
    shapes = [(CAP, part), (CAP, part * 3 // 2), (CAP, part * 3 // 2)]
    return pl.pallas_call(
        select_kernel,
        grid_spec=pltpu.PrefetchScalarGridSpec(
            num_scalar_prefetch=1,
            grid=(X,),
            in_specs=[
                whole((1, tokens)),
                whole((1, tokens)),
                pl.BlockSpec((tokens, part), lambda k, w: (0, lax.rem(w[1] + k, X))),
            ],
            out_specs=[whole(shape) for shape in shapes] + [whole((CAP, 128))],
            scratch_shapes=[pltpu.VMEM((CAP, tokens), BF16)],
        ),
        out_shape=[jax.ShapeDtypeStruct(shape, BF16) for shape in shapes]
        + [jax.ShapeDtypeStruct((CAP, 128), F32)],
        compiler_params=params(),
        cost_estimate=cost(2 * CAP * tokens * width, 2 * tokens * width),
    )(where, ids, label, hidden)


def project_first_kernel(offsets, *refs):
    rows, chunks, out = refs[:X], refs[X : X + len(offsets)], refs[-1]
    depth = chunks[0].shape[0]
    part = depth * Z
    left = jnp.concatenate([r[:, :part] for r in rows], axis=0)
    total = None
    for offset, chunk in zip(offsets, chunks):
        term = jnp.dot(
            left[:, offset * depth : (offset + 1) * depth],
            chunk[...],
            preferred_element_type=F32,
        )
        total = term if total is None else total + term
    out[...] = total


def project_first(rows, chunks, offsets):
    depth, wide = chunks[0].shape
    return pl.pallas_call(
        lambda *refs: project_first_kernel(offsets, *refs),
        out_shape=jax.ShapeDtypeStruct((X * CAP, wide), F32),
        compiler_params=params(),
        cost_estimate=cost(2 * X * CAP * depth * len(chunks) * wide, 6_000_000),
    )(*rows, *chunks)


def project_last_kernel(total_ref, *refs):
    rows, front, back, outs = refs[:X], refs[X], refs[X + 1], refs[X + 2 :]
    half = front.shape[0]
    left = jnp.concatenate([r[...] for r in rows], axis=0)
    total = total_ref[...]
    total += jnp.dot(left[:, :half], front[...], preferred_element_type=F32)
    total += jnp.dot(left[:, half:], back[...], preferred_element_type=F32)
    for k in range(X):
        outs[k][...] = total[k * CAP : (k + 1) * CAP, :].astype(outs[k].dtype)


def project_last(total, rows, front, back, held):
    half, wide = front.shape
    depth = 2 * half
    at = lambda *index: lambda i: index
    return pl.pallas_call(
        project_last_kernel,
        grid=(1,),
        in_specs=[pl.BlockSpec(total.shape, at(0, 0))]
        + [pl.BlockSpec((CAP, depth), at(0, Z // 2))] * X
        + [pl.BlockSpec((half, wide), at(0, 0))] * 2,
        out_specs=[pl.BlockSpec((CAP, wide), at(0, 0))] * X,
        out_shape=[jax.ShapeDtypeStruct((CAP, wide), held)] * X,
        compiler_params=params(),
        cost_estimate=cost(2 * X * CAP * depth * wide, 3_000_000),
    )(total, *rows, front, back)


FIRST = (0, 1, 7, 2, 6)
SECOND = (3, 5, 4)


def word_kernel(last, blocks, where_ref, both_ref, word_ref, *refs):
    tables, refs = refs[: X + 1], refs[X + 1 :]
    before = refs[0] if last else None
    out_ref = refs[-1]
    x, z = where_ref[1], where_ref[2]
    rows = word_ref.shape[0]
    deep, width = tables[0].shape
    half = deep // 2

    codes = word_ref[...]
    word = (codes[:, 0:1] * 128.0 + codes[:, 1:2]).astype(jnp.int32)
    column = lax.broadcasted_iota(jnp.int32, (rows, 128), 1)
    best = total = hit = None
    for part, back in enumerate((0, 1, 3, 2)):
        if part < X - 1:
            products = jnp.dot(
                both_ref[...], tables[part][:deep, :], preferred_element_type=F32
            )
        else:
            products = jnp.dot(
                both_ref[:, :half], tables[part][...], preferred_element_type=F32
            )
            products += jnp.dot(
                both_ref[:, half:], tables[part + 1][...], preferred_element_type=F32
            )
        logits = products[:rows] + products[rows:]
        local = word - (lax.rem(x - back + X, X) * Z + z) * width
        tiles = [logits[:, i * 128 : (i + 1) * 128] for i in range(width // 128)]
        peak = tiles[0]
        for tile in tiles[1:]:
            peak = jnp.maximum(peak, tile)
        if best is None:
            best, total, hit = peak, jnp.zeros_like(peak), jnp.zeros_like(peak)
        else:
            peak = jnp.maximum(best, peak)
            best, total = peak, total * jnp.exp(best - peak)
        for i, tile in enumerate(tiles):
            total += jnp.exp(tile - best)
            hit += jnp.where(column + i * 128 == local, tile, 0.0)

    highest = jnp.max(best, axis=1, keepdims=True)
    summed = jnp.sum(total * jnp.exp(best - highest), axis=1, keepdims=True)
    chosen = jnp.sum(hit, axis=1, keepdims=True)
    stats = jnp.where(
        column == 0,
        highest,
        jnp.where(column == 1, summed, jnp.where(column == 2, chosen, 0.0)),
    )
    for i, back in enumerate(blocks):
        piece = stats[i * CAP : (i + 1) * CAP, :]
        turned = jnp.concatenate([piece, piece], axis=0).T
        top_sum = jnp.where(column[0:1] < CAP, turned[0:1], turned[1:2])
        pair = jnp.concatenate([top_sum, turned[2:3]], axis=0)
        if last:
            for s in range(SECTIONS):
                out_ref[s, lax.rem(z - back + Z, Z)] = pair
        else:
            out_ref[i] = pair
    if last:
        for i, back in enumerate(FIRST):
            for s in range(SECTIONS):
                out_ref[s, lax.rem(z - back + Z, Z)] = before[i]


def word_stats(where, both, words, tables, before=None):
    last = before is not None
    blocks = SECOND if last else FIRST
    rows, depth = words.shape[0], both.shape[1]
    width = tables[0].shape[1]
    inside = pl.BlockSpec(memory_space=pltpu.VMEM)
    return pl.pallas_call(
        lambda *refs: word_kernel(last, blocks, *refs),
        in_specs=[pl.BlockSpec(memory_space=pltpu.SMEM), inside, inside]
        + [inside] * (X + 1)
        + ([inside] if last else []),
        out_specs=inside,
        out_shape=jax.ShapeDtypeStruct(
            ((SECTIONS, Z) if last else (len(blocks),)) + (2, 128), F32
        ),
        compiler_params=params(),
        cost_estimate=cost(4 * rows * depth * width * X, 2 * depth * width * X),
    )(where, both, words, *tables, *((before,) if last else ()))


def combine_kernel(ids_ref, stats_ref, out_ref):
    stats = stats_ref[...]
    tokens = ids_ref.shape[1]
    top, total, chosen = stats[:, :, 0, :CAP], stats[:, :, 0, CAP:], stats[:, :, 1, :CAP]
    highest = jnp.max(top, axis=1, keepdims=True)
    summed = jnp.sum(total * jnp.exp(top - highest), axis=1)
    loss = highest[:, 0] + jnp.log(summed) - jnp.sum(chosen, axis=1)
    columns = jnp.concatenate(
        [
            jnp.concatenate([loss, jnp.zeros((SECTIONS, 128 - CAP), F32)], axis=1),
            jnp.zeros((128 - SECTIONS, 128), F32),
        ],
        axis=0,
    ).T
    ids = ids_ref[...]
    owner = lax.broadcasted_iota(jnp.int32, (SECTIONS, tokens), 0)
    mine = jnp.where(ids == owner, 1.0, 0.0).astype(F32)
    earlier = lax.broadcasted_iota(jnp.int32, (tokens, tokens), 0)
    later = lax.broadcasted_iota(jnp.int32, (tokens, tokens), 1)
    upto = jnp.where(earlier <= later, 1.0, 0.0).astype(F32)
    within = jnp.dot(mine, upto, preferred_element_type=F32)
    slot = jnp.sum(within * mine, axis=0, keepdims=True)
    slot = (slot + 0.5).astype(jnp.int32) - 1
    place = lax.broadcasted_iota(jnp.int32, (CAP, tokens), 0)
    found = jnp.zeros((CAP, tokens), F32)
    for s in range(SECTIONS):
        found = jnp.where(ids == s, columns[0:CAP, s : s + 1], found)
    out_ref[...] = jnp.sum(jnp.where(place == slot, found, 0.0), axis=0, keepdims=True)


def combine(ids, stats):
    tokens = ids.shape[1]
    return pl.pallas_call(
        combine_kernel,
        out_shape=jax.ShapeDtypeStruct((1, tokens), F32),
        compiler_params=params(),
        cost_estimate=cost(2 * 8 * tokens * tokens, 400_000),
    )(ids, stats)


def split(blocks, width):
    held = jnp.concatenate(blocks, axis=0)
    wide = held[:, :width].astype(F32)
    high = lax.reduce_precision(wide, exponent_bits=8, mantissa_bits=7)
    both = jnp.concatenate([high, wide - high], axis=0).astype(BF16)
    return both, held[:, width:].astype(F32)


def relay(table, message, part):
    width = table.shape[1]
    return jnp.concatenate(
        [table, message[:, part : part + width], message[:, part + width :]], axis=0
    )


def body(hidden, cluster, label, proj, emb):
    x, z = lax.axis_index("x"), lax.axis_index("z")
    owner = lax.axis_index("y") * 2 + lax.axis_index("core")
    where = jnp.stack([owner, x, z]).astype(jnp.int32)
    ids = cluster.reshape(1, -1)
    weight, table = proj[0], emb[0]
    half = weight.shape[0] // 2
    wide = weight.shape[1]
    middle = table.shape[0] // 2

    deep = table.shape[0]
    right1, left1 = ring(weight, "z", Z, 1), ring(weight, "z", Z, -1)
    own_rows, up, down, words = select_rows(where, ids, label.reshape(1, -1), hidden)
    part = own_rows.shape[1]
    up, down = ring(up, "x", X, 1), ring(down, "x", X, -1)
    right1, left1, words = lax.optimization_barrier((right1, left1, words))
    right2, left2 = ring(right1, "z", Z, 1), ring(left1, "z", Z, -1)
    up, down, _, _ = lax.optimization_barrier((up, down, right1, left1))
    after = ring(relay(table, up, part), "x", X, 1)
    ahead = ring(relay(table, down, part), "x", X, -1)
    right3, left3 = ring(right2, "z", Z, 1), ring(left2, "z", Z, -1)
    front = ring(right3[:half], "z", Z, 1)
    back = ring(left3[half:], "z", Z, -1)
    front, back, after, ahead = lax.optimization_barrier((front, back, after, ahead))
    far1 = ring(after[:middle], "x", X, 1)
    far2 = ring(ahead[middle:deep], "x", X, -1)
    tables = [table, after, ahead, far1, far2]
    across = jnp.concatenate(
        [side[deep + i : deep + i + CAP] for side in (after, ahead) for i in (0, CAP)],
        axis=1,
    )
    rows = [own_rows, up, across, down]

    chunks = [weight, right1, left1, right2, left2, right3, left3]
    total = project_first(rows, chunks, [0, 7, 1, 6, 2, 5, 3])
    parts = project_last(total, rows, front, back, F32)
    own = parts[0]
    for k in range(1, X):
        own = own + ring(parts[k].astype(F16), "x", X, -k).astype(F32)

    message = jnp.concatenate([own, words], axis=1).astype(F16)
    r1, l1 = ring(message, "z", Z, 1), ring(message, "z", Z, -1)
    r2, l2 = ring(message, "z", Z, 2), ring(message, "z", Z, -2)
    r3, l3 = ring(r2, "z", Z, 1), ring(l2, "z", Z, -1)
    r4 = ring(r2, "z", Z, 2)

    stats = word_stats(where, *split([message, r1, l1, r2, l2], wide), tables)
    stats, r3, l3, r4 = lax.optimization_barrier((stats, r3, l3, r4))
    stats = word_stats(where, *split([r3, l3, r4], wide), tables, stats)
    stats = stats.reshape(SECTIONS * Z, 2, 128)
    stats = lax.all_to_all(stats, ("y", "core", "z"), 0, 0, tiled=True)
    loss = combine(ids, stats.reshape(SECTIONS, Z, 2, 128))
    return loss.reshape(-1)


def solution(mesh):
    fine = Mesh(mesh.devices.reshape(4, 2, X, Z), ("y", "core", "x", "z"))
    return jax.shard_map(
        body,
        mesh=fine,
        in_specs=(
            P(("x", "z"), None),
            P(("x", "z"), None),
            P(("x", "z")),
            P(("y", "core"), ("x", "z"), None),
            P(("y", "core"), None, ("x", "z")),
        ),
        out_specs=P(("x", "z")),
        check_vma=False,
    )
```

```python
import jax
import jax.numpy as jnp
from jax import lax
from jax.experimental import pallas as pl
from jax.experimental.pallas import tpu as pltpu
from jax.sharding import Mesh
from jax.sharding import PartitionSpec as P

CAP = 64
X = 4
Z = 8
SECTIONS = 8
BF16 = jnp.bfloat16
F16 = jnp.float16
F32 = jnp.float32
VMEM_LIMIT = 40 * 1024 * 1024


def ring(array, axis, size, step):
    return lax.ppermute(array, axis, [(i, (i + step) % size) for i in range(size)])


def params():
    return pltpu.CompilerParams(vmem_limit_bytes=VMEM_LIMIT)


def cost(flops, moved):
    return pl.CostEstimate(flops=flops, bytes_accessed=moved, transcendentals=0)


def slot_choice(ids, owner):
    tokens = ids.shape[1]
    mine = ids == owner
    ones = jnp.where(mine, 1.0, 0.0).astype(F32)
    earlier = lax.broadcasted_iota(jnp.int32, (tokens, tokens), 0)
    later = lax.broadcasted_iota(jnp.int32, (tokens, tokens), 1)
    upto = jnp.where(earlier <= later, 1.0, 0.0).astype(F32)
    within = jnp.dot(
        jnp.broadcast_to(ones, (8, tokens)), upto, preferred_element_type=F32
    )[0:1, :]
    place = lax.broadcasted_iota(jnp.int32, (CAP, tokens), 0)
    within = (within + 0.5).astype(jnp.int32) - 1
    return (within == place) & mine


def select_kernel(
    where_ref, ids_ref, label_ref, hidden_ref, own_ref, up_ref, down_ref, words_ref, choice_ref
):
    owner, z = where_ref[0], where_ref[2]
    step = pl.program_id(0)

    @pl.when(step == 0)
    def _():
        choice = slot_choice(ids_ref[...], owner)
        choice_ref[...] = jnp.where(choice, 1.0, 0.0).astype(BF16)
        word = jnp.sum(jnp.where(choice, label_ref[...], 0), axis=1, keepdims=True)
        lane = lax.broadcasted_iota(jnp.int32, (CAP, 128), 1)
        parts = jnp.where(lane == 0, word >> 7, jnp.where(lane == 1, word & 127, 0))
        words_ref[...] = parts.astype(F32)

    part = hidden_ref.shape[1]
    depth, half = part // Z, part // 2

    def pick(j):
        at = pl.multiple_of(lax.rem(z + j, Z) * depth, depth)
        rows = jnp.dot(
            choice_ref[...], hidden_ref[:, pl.ds(at, depth)], preferred_element_type=F32
        )
        return rows.astype(BF16)

    for k, target in enumerate((own_ref, up_ref, None, down_ref)):

        @pl.when(step == k)
        def _(target=target):
            for j in range(Z):
                at = j * depth
                if target is not None:
                    target[:, at : at + depth] = pick(j)
                elif at < half:
                    up_ref[:, part + at : part + at + depth] = pick(j)
                else:
                    down_ref[:, half + at : half + at + depth] = pick(j)


def select_rows(where, ids, label, hidden):
    tokens, width = hidden.shape
    part = width // X
    whole = lambda shape: pl.BlockSpec(shape, lambda k, w: (0, 0))
    shapes = [(CAP, part), (CAP, part * 3 // 2), (CAP, part * 3 // 2)]
    return pl.pallas_call(
        select_kernel,
        grid_spec=pltpu.PrefetchScalarGridSpec(
            num_scalar_prefetch=1,
            grid=(X,),
            in_specs=[
                whole((1, tokens)),
                whole((1, tokens)),
                pl.BlockSpec((tokens, part), lambda k, w: (0, lax.rem(w[1] + k, X))),
            ],
            out_specs=[whole(shape) for shape in shapes] + [whole((CAP, 128))],
            scratch_shapes=[pltpu.VMEM((CAP, tokens), BF16)],
        ),
        out_shape=[jax.ShapeDtypeStruct(shape, BF16) for shape in shapes]
        + [jax.ShapeDtypeStruct((CAP, 128), F32)],
        compiler_params=params(),
        cost_estimate=cost(2 * CAP * tokens * width, 2 * tokens * width),
    )(where, ids, label, hidden)


def project_first_kernel(offsets, *refs):
    rows, chunks, out = refs[:X], refs[X : X + len(offsets)], refs[-1]
    depth = chunks[0].shape[0]
    part = depth * Z
    left = jnp.concatenate([r[:, :part] for r in rows], axis=0)
    total = None
    for offset, chunk in zip(offsets, chunks):
        term = jnp.dot(
            left[:, offset * depth : (offset + 1) * depth],
            chunk[...],
            preferred_element_type=F32,
        )
        total = term if total is None else total + term
    out[...] = total


def project_first(rows, chunks, offsets):
    depth, wide = chunks[0].shape
    return pl.pallas_call(
        lambda *refs: project_first_kernel(offsets, *refs),
        out_shape=jax.ShapeDtypeStruct((X * CAP, wide), F32),
        compiler_params=params(),
        cost_estimate=cost(2 * X * CAP * depth * len(chunks) * wide, 6_000_000),
    )(*rows, *chunks)


def project_last_kernel(total_ref, *refs):
    rows, front, back, outs = refs[:X], refs[X], refs[X + 1], refs[X + 2 :]
    half = front.shape[0]
    left = jnp.concatenate([r[...] for r in rows], axis=0)
    total = total_ref[...]
    total += jnp.dot(left[:, :half], front[...], preferred_element_type=F32)
    total += jnp.dot(left[:, half:], back[...], preferred_element_type=F32)
    for k in range(X):
        outs[k][...] = total[k * CAP : (k + 1) * CAP, :].astype(outs[k].dtype)


def project_last(total, rows, front, back, held):
    half, wide = front.shape
    depth = 2 * half
    at = lambda *index: lambda i: index
    return pl.pallas_call(
        project_last_kernel,
        grid=(1,),
        in_specs=[pl.BlockSpec(total.shape, at(0, 0))]
        + [pl.BlockSpec((CAP, depth), at(0, Z // 2))] * X
        + [pl.BlockSpec((half, wide), at(0, 0))] * 2,
        out_specs=[pl.BlockSpec((CAP, wide), at(0, 0))] * X,
        out_shape=[jax.ShapeDtypeStruct((CAP, wide), held)] * X,
        compiler_params=params(),
        cost_estimate=cost(2 * X * CAP * depth * wide, 3_000_000),
    )(total, *rows, front, back)


FIRST = (0, 1, 7, 2, 6)
SECOND = (3, 5, 4)


def word_kernel(last, blocks, where_ref, both_ref, word_ref, *refs):
    tables, refs = refs[: X + 1], refs[X + 1 :]
    before = refs[0] if last else None
    out_ref = refs[-1]
    x, z = where_ref[1], where_ref[2]
    rows = word_ref.shape[0]
    deep, width = tables[0].shape
    half = deep // 2

    codes = word_ref[...]
    word = (codes[:, 0:1] * 128.0 + codes[:, 1:2]).astype(jnp.int32)
    column = lax.broadcasted_iota(jnp.int32, (rows, 128), 1)
    best = total = hit = None
    for part, back in enumerate((0, 1, 3, 2)):
        if part < X - 1:
            products = jnp.dot(
                both_ref[...], tables[part][:deep, :], preferred_element_type=F32
            )
        else:
            products = jnp.dot(
                both_ref[:, :half], tables[part][...], preferred_element_type=F32
            )
            products += jnp.dot(
                both_ref[:, half:], tables[part + 1][...], preferred_element_type=F32
            )
        logits = products[:rows] + products[rows:]
        local = word - (lax.rem(x - back + X, X) * Z + z) * width
        tiles = [logits[:, i * 128 : (i + 1) * 128] for i in range(width // 128)]
        peak = tiles[0]
        for tile in tiles[1:]:
            peak = jnp.maximum(peak, tile)
        if best is None:
            best, total, hit = peak, jnp.zeros_like(peak), jnp.zeros_like(peak)
        else:
            peak = jnp.maximum(best, peak)
            best, total = peak, total * jnp.exp(best - peak)
        for i, tile in enumerate(tiles):
            total += jnp.exp(tile - best)
            hit += jnp.where(column + i * 128 == local, tile, 0.0)

    highest = jnp.max(best, axis=1, keepdims=True)
    summed = jnp.sum(total * jnp.exp(best - highest), axis=1, keepdims=True)
    chosen = jnp.sum(hit, axis=1, keepdims=True)
    stats = jnp.where(
        column == 0,
        highest,
        jnp.where(column == 1, summed, jnp.where(column == 2, chosen, 0.0)),
    )
    for i, back in enumerate(blocks):
        piece = stats[i * CAP : (i + 1) * CAP, :]
        turned = jnp.concatenate([piece, piece], axis=0).T
        top_sum = jnp.where(column[0:1] < CAP, turned[0:1], turned[1:2])
        pair = jnp.concatenate([top_sum, turned[2:3]], axis=0)
        if last:
            for s in range(SECTIONS):
                out_ref[s, lax.rem(z - back + Z, Z)] = pair
        else:
            out_ref[i] = pair
    if last:
        for i, back in enumerate(FIRST):
            for s in range(SECTIONS):
                out_ref[s, lax.rem(z - back + Z, Z)] = before[i]


def word_stats(where, both, words, tables, before=None):
    last = before is not None
    blocks = SECOND if last else FIRST
    rows, depth = words.shape[0], both.shape[1]
    width = tables[0].shape[1]
    inside = pl.BlockSpec(memory_space=pltpu.VMEM)
    return pl.pallas_call(
        lambda *refs: word_kernel(last, blocks, *refs),
        in_specs=[pl.BlockSpec(memory_space=pltpu.SMEM), inside, inside]
        + [inside] * (X + 1)
        + ([inside] if last else []),
        out_specs=inside,
        out_shape=jax.ShapeDtypeStruct(
            ((SECTIONS, Z) if last else (len(blocks),)) + (2, 128), F32
        ),
        compiler_params=params(),
        cost_estimate=cost(4 * rows * depth * width * X, 2 * depth * width * X),
    )(where, both, words, *tables, *((before,) if last else ()))


def combine_kernel(ids_ref, stats_ref, out_ref):
    stats = stats_ref[...]
    tokens = ids_ref.shape[1]
    top, total, chosen = stats[:, :, 0, :CAP], stats[:, :, 0, CAP:], stats[:, :, 1, :CAP]
    highest = jnp.max(top, axis=1, keepdims=True)
    summed = jnp.sum(total * jnp.exp(top - highest), axis=1)
    loss = highest[:, 0] + jnp.log(summed) - jnp.sum(chosen, axis=1)
    columns = jnp.concatenate(
        [
            jnp.concatenate([loss, jnp.zeros((SECTIONS, 128 - CAP), F32)], axis=1),
            jnp.zeros((128 - SECTIONS, 128), F32),
        ],
        axis=0,
    ).T
    ids = ids_ref[...]
    owner = lax.broadcasted_iota(jnp.int32, (SECTIONS, tokens), 0)
    mine = jnp.where(ids == owner, 1.0, 0.0).astype(F32)
    earlier = lax.broadcasted_iota(jnp.int32, (tokens, tokens), 0)
    later = lax.broadcasted_iota(jnp.int32, (tokens, tokens), 1)
    upto = jnp.where(earlier <= later, 1.0, 0.0).astype(F32)
    within = jnp.dot(mine, upto, preferred_element_type=F32)
    slot = jnp.sum(within * mine, axis=0, keepdims=True)
    slot = (slot + 0.5).astype(jnp.int32) - 1
    place = lax.broadcasted_iota(jnp.int32, (CAP, tokens), 0)
    found = jnp.zeros((CAP, tokens), F32)
    for s in range(SECTIONS):
        found = jnp.where(ids == s, columns[0:CAP, s : s + 1], found)
    out_ref[...] = jnp.sum(jnp.where(place == slot, found, 0.0), axis=0, keepdims=True)


def combine(ids, stats):
    tokens = ids.shape[1]
    return pl.pallas_call(
        combine_kernel,
        out_shape=jax.ShapeDtypeStruct((1, tokens), F32),
        compiler_params=params(),
        cost_estimate=cost(2 * 8 * tokens * tokens, 400_000),
    )(ids, stats)


def split(blocks, width):
    held = jnp.concatenate(blocks, axis=0)
    wide = held[:, :width].astype(F32)
    high = lax.reduce_precision(wide, exponent_bits=8, mantissa_bits=7)
    both = jnp.concatenate([high, wide - high], axis=0).astype(BF16)
    return both, held[:, width:].astype(F32)


def relay(table, message, part):
    width = table.shape[1]
    return jnp.concatenate(
        [table, message[:, part : part + width], message[:, part + width :]], axis=0
    )


def body(hidden, cluster, label, proj, emb):
    x, z = lax.axis_index("x"), lax.axis_index("z")
    owner = lax.axis_index("y") * 2 + lax.axis_index("core")
    where = jnp.stack([owner, x, z]).astype(jnp.int32)
    ids = cluster.reshape(1, -1)
    weight, table = proj[0], emb[0]
    half = weight.shape[0] // 2
    wide = weight.shape[1]
    middle = table.shape[0] // 2

    deep = table.shape[0]
    right1, left1 = ring(weight, "z", Z, 1), ring(weight, "z", Z, -1)
    own_rows, up, down, words = select_rows(where, ids, label.reshape(1, -1), hidden)
    part = own_rows.shape[1]
    up, down = ring(up, "x", X, 1), ring(down, "x", X, -1)
    right1, left1, words = lax.optimization_barrier((right1, left1, words))
    right2, left2 = ring(right1, "z", Z, 1), ring(left1, "z", Z, -1)
    up, down, _, _ = lax.optimization_barrier((up, down, right1, left1))
    after = ring(relay(table, up, part), "x", X, 1)
    ahead = ring(relay(table, down, part), "x", X, -1)
    right3, left3 = ring(right2, "z", Z, 1), ring(left2, "z", Z, -1)
    front = ring(right3[:half], "z", Z, 1)
    back = ring(left3[half:], "z", Z, -1)
    front, back, after, ahead = lax.optimization_barrier((front, back, after, ahead))
    far1 = ring(after[:middle], "x", X, 1)
    far2 = ring(ahead[middle:deep], "x", X, -1)
    tables = [table, after, ahead, far1, far2]
    across = jnp.concatenate(
        [side[deep + i : deep + i + CAP] for side in (after, ahead) for i in (0, CAP)],
        axis=1,
    )
    rows = [own_rows, up, across, down]

    chunks = [weight, right1, left1, right2, left2, right3, left3]
    total = project_first(rows, chunks, [0, 7, 1, 6, 2, 5, 3])
    parts = project_last(total, rows, front, back, F32)
    own = parts[0]
    for k in range(1, X):
        own = own + ring(parts[k].astype(F16), "x", X, -k).astype(F32)

    message = jnp.concatenate([own, words], axis=1).astype(F16)
    r1, l1 = ring(message, "z", Z, 1), ring(message, "z", Z, -1)
    r2, l2 = ring(message, "z", Z, 2), ring(message, "z", Z, -2)
    r3, l3 = ring(r2, "z", Z, 1), ring(l2, "z", Z, -1)
    edge = CAP // 2
    r4, l4 = ring(r2[:edge], "z", Z, 2), ring(l2[edge:], "z", Z, -2)

    stats = word_stats(where, *split([message, r1, l1, r2, l2], wide), tables)
    stats, r3, l3, r4, l4 = lax.optimization_barrier((stats, r3, l3, r4, l4))
    stats = word_stats(where, *split([r3, l3, r4, l4], wide), tables, stats)
    stats = stats.reshape(SECTIONS * Z, 2, 128)
    stats = lax.all_to_all(stats, ("y", "core", "z"), 0, 0, tiled=True)
    loss = combine(ids, stats.reshape(SECTIONS, Z, 2, 128))
    return loss.reshape(-1)


def solution(mesh):
    fine = Mesh(mesh.devices.reshape(4, 2, X, Z), ("y", "core", "x", "z"))
    return jax.shard_map(
        body,
        mesh=fine,
        in_specs=(
            P(("x", "z"), None),
            P(("x", "z"), None),
            P(("x", "z")),
            P(("y", "core"), ("x", "z"), None),
            P(("y", "core"), None, ("x", "z")),
        ),
        out_specs=P(("x", "z")),
        check_vma=False,
    )
```

```python
import jax
import jax.numpy as jnp
from jax import lax
from jax.experimental import pallas as pl
from jax.experimental.pallas import tpu as pltpu
from jax.sharding import Mesh
from jax.sharding import PartitionSpec as P

CAP = 64
X = 4
Z = 8
SECTIONS = 8
BF16 = jnp.bfloat16
F16 = jnp.float16
F32 = jnp.float32
VMEM_LIMIT = 40 * 1024 * 1024


def ring(array, axis, size, step):
    return lax.ppermute(array, axis, [(i, (i + step) % size) for i in range(size)])


def params():
    return pltpu.CompilerParams(vmem_limit_bytes=VMEM_LIMIT)


def cost(flops, moved):
    return pl.CostEstimate(flops=flops, bytes_accessed=moved, transcendentals=0)


def slot_choice(ids, owner):
    tokens = ids.shape[1]
    mine = ids == owner
    ones = jnp.where(mine, 1.0, 0.0).astype(F32)
    earlier = lax.broadcasted_iota(jnp.int32, (tokens, tokens), 0)
    later = lax.broadcasted_iota(jnp.int32, (tokens, tokens), 1)
    upto = jnp.where(earlier <= later, 1.0, 0.0).astype(F32)
    within = jnp.dot(
        jnp.broadcast_to(ones, (8, tokens)), upto, preferred_element_type=F32
    )[0:1, :]
    place = lax.broadcasted_iota(jnp.int32, (CAP, tokens), 0)
    within = (within + 0.5).astype(jnp.int32) - 1
    return (within == place) & mine


def select_kernel(
    where_ref, ids_ref, label_ref, hidden_ref, own_ref, up_ref, down_ref, words_ref, choice_ref
):
    owner, z = where_ref[0], where_ref[2]
    step = pl.program_id(0)

    @pl.when(step == 0)
    def _():
        choice = slot_choice(ids_ref[...], owner)
        choice_ref[...] = jnp.where(choice, 1.0, 0.0).astype(BF16)
        word = jnp.sum(jnp.where(choice, label_ref[...], 0), axis=1, keepdims=True)
        lane = lax.broadcasted_iota(jnp.int32, (CAP, 128), 1)
        parts = jnp.where(lane == 0, word >> 7, jnp.where(lane == 1, word & 127, 0))
        words_ref[...] = parts.astype(F32)

    part = hidden_ref.shape[1]
    depth, half = part // Z, part // 2

    def pick(j):
        at = pl.multiple_of(lax.rem(z + j, Z) * depth, depth)
        rows = jnp.dot(
            choice_ref[...], hidden_ref[:, pl.ds(at, depth)], preferred_element_type=F32
        )
        return rows.astype(BF16)

    for k, target in enumerate((own_ref, up_ref, None, down_ref)):

        @pl.when(step == k)
        def _(target=target):
            for j in range(Z):
                at = j * depth
                if target is not None:
                    target[:, at : at + depth] = pick(j)
                elif at < half:
                    up_ref[:, part + at : part + at + depth] = pick(j)
                else:
                    down_ref[:, half + at : half + at + depth] = pick(j)


def select_rows(where, ids, label, hidden):
    tokens, width = hidden.shape
    part = width // X
    whole = lambda shape: pl.BlockSpec(shape, lambda k, w: (0, 0))
    shapes = [(CAP, part), (CAP, part * 3 // 2), (CAP, part * 3 // 2)]
    return pl.pallas_call(
        select_kernel,
        grid_spec=pltpu.PrefetchScalarGridSpec(
            num_scalar_prefetch=1,
            grid=(X,),
            in_specs=[
                whole((1, tokens)),
                whole((1, tokens)),
                pl.BlockSpec((tokens, part), lambda k, w: (0, lax.rem(w[1] + k, X))),
            ],
            out_specs=[whole(shape) for shape in shapes] + [whole((CAP, 128))],
            scratch_shapes=[pltpu.VMEM((CAP, tokens), BF16)],
        ),
        out_shape=[jax.ShapeDtypeStruct(shape, BF16) for shape in shapes]
        + [jax.ShapeDtypeStruct((CAP, 128), F32)],
        compiler_params=params(),
        cost_estimate=cost(2 * CAP * tokens * width, 2 * tokens * width),
    )(where, ids, label, hidden)


def project_first_kernel(offsets, *refs):
    rows, chunks, out = refs[:X], refs[X : X + len(offsets)], refs[-1]
    depth = chunks[0].shape[0]
    part = depth * Z
    left = jnp.concatenate([r[:, :part] for r in rows], axis=0)
    total = None
    for offset, chunk in zip(offsets, chunks):
        term = jnp.dot(
            left[:, offset * depth : (offset + 1) * depth],
            chunk[...],
            preferred_element_type=F32,
        )
        total = term if total is None else total + term
    out[...] = total


def project_first(rows, chunks, offsets):
    depth, wide = chunks[0].shape
    return pl.pallas_call(
        lambda *refs: project_first_kernel(offsets, *refs),
        out_shape=jax.ShapeDtypeStruct((X * CAP, wide), F32),
        compiler_params=params(),
        cost_estimate=cost(2 * X * CAP * depth * len(chunks) * wide, 6_000_000),
    )(*rows, *chunks)


def project_last_kernel(total_ref, *refs):
    rows, front, back, outs = refs[:X], refs[X], refs[X + 1], refs[X + 2 :]
    half = front.shape[0]
    left = jnp.concatenate([r[...] for r in rows], axis=0)
    total = total_ref[...]
    total += jnp.dot(left[:, :half], front[...], preferred_element_type=F32)
    total += jnp.dot(left[:, half:], back[...], preferred_element_type=F32)
    for k in range(X):
        outs[k][...] = total[k * CAP : (k + 1) * CAP, :].astype(outs[k].dtype)


def project_last(total, rows, front, back, held):
    half, wide = front.shape
    depth = 2 * half
    at = lambda *index: lambda i: index
    return pl.pallas_call(
        project_last_kernel,
        grid=(1,),
        in_specs=[pl.BlockSpec(total.shape, at(0, 0))]
        + [pl.BlockSpec((CAP, depth), at(0, Z // 2))] * X
        + [pl.BlockSpec((half, wide), at(0, 0))] * 2,
        out_specs=[pl.BlockSpec((CAP, wide), at(0, 0))] * X,
        out_shape=[jax.ShapeDtypeStruct((CAP, wide), held)] * X,
        compiler_params=params(),
        cost_estimate=cost(2 * X * CAP * depth * wide, 3_000_000),
    )(total, *rows, front, back)


FIRST = (0, 1, 7, 2, 6)
SECOND = (3, 5, 4)


def word_kernel(last, blocks, where_ref, both_ref, word_ref, *refs):
    tables, refs = refs[: X + 1], refs[X + 1 :]
    before = refs[0] if last else None
    out_ref = refs[-1]
    x, z = where_ref[1], where_ref[2]
    rows = word_ref.shape[0]
    deep, width = tables[0].shape
    half = deep // 2

    codes = word_ref[...]
    word = (codes[:, 0:1] * 128.0 + codes[:, 1:2]).astype(jnp.int32)
    column = lax.broadcasted_iota(jnp.int32, (rows, 128), 1)
    best = total = hit = None
    for part, back in enumerate((0, 1, 3, 2)):
        if part < X - 1:
            products = jnp.dot(
                both_ref[...], tables[part][:deep, :], preferred_element_type=F32
            )
        else:
            products = jnp.dot(
                both_ref[:, :half], tables[part][...], preferred_element_type=F32
            )
            products += jnp.dot(
                both_ref[:, half:], tables[part + 1][...], preferred_element_type=F32
            )
        logits = products[:rows] + products[rows:]
        local = word - (lax.rem(x - back + X, X) * Z + z) * width
        tiles = [logits[:, i * 128 : (i + 1) * 128] for i in range(width // 128)]
        peak = tiles[0]
        for tile in tiles[1:]:
            peak = jnp.maximum(peak, tile)
        if best is None:
            best, total, hit = peak, jnp.zeros_like(peak), jnp.zeros_like(peak)
        else:
            peak = jnp.maximum(best, peak)
            best, total = peak, total * jnp.exp(best - peak)
        for i, tile in enumerate(tiles):
            total += jnp.exp(tile - best)
            hit += jnp.where(column + i * 128 == local, tile, 0.0)

    highest = jnp.max(best, axis=1, keepdims=True)
    summed = jnp.sum(total * jnp.exp(best - highest), axis=1, keepdims=True)
    chosen = jnp.sum(hit, axis=1, keepdims=True)
    stats = jnp.where(
        column == 0,
        highest,
        jnp.where(column == 1, summed, jnp.where(column == 2, chosen, 0.0)),
    )
    for i, back in enumerate(blocks):
        piece = stats[i * CAP : (i + 1) * CAP, :]
        turned = jnp.concatenate([piece, piece], axis=0).T
        top_sum = jnp.where(column[0:1] < CAP, turned[0:1], turned[1:2])
        pair = jnp.concatenate([top_sum, turned[2:3]], axis=0)
        if last:
            for s in range(SECTIONS):
                out_ref[s, lax.rem(z - back + Z, Z)] = pair
        else:
            out_ref[i] = pair
    if last:
        for i, back in enumerate(FIRST):
            for s in range(SECTIONS):
                out_ref[s, lax.rem(z - back + Z, Z)] = before[i]


def word_stats(where, both, words, tables, before=None):
    last = before is not None
    blocks = SECOND if last else FIRST
    rows, depth = words.shape[0], both.shape[1]
    width = tables[0].shape[1]
    inside = pl.BlockSpec(memory_space=pltpu.VMEM)
    return pl.pallas_call(
        lambda *refs: word_kernel(last, blocks, *refs),
        in_specs=[pl.BlockSpec(memory_space=pltpu.SMEM), inside, inside]
        + [inside] * (X + 1)
        + ([inside] if last else []),
        out_specs=inside,
        out_shape=jax.ShapeDtypeStruct(
            ((SECTIONS, Z) if last else (len(blocks),)) + (2, 128), F32
        ),
        compiler_params=params(),
        cost_estimate=cost(4 * rows * depth * width * X, 2 * depth * width * X),
    )(where, both, words, *tables, *((before,) if last else ()))


def combine_kernel(ids_ref, stats_ref, out_ref):
    stats = stats_ref[...]
    tokens = ids_ref.shape[1]
    top, total, chosen = stats[:, :, 0, :CAP], stats[:, :, 0, CAP:], stats[:, :, 1, :CAP]
    highest = jnp.max(top, axis=1, keepdims=True)
    summed = jnp.sum(total * jnp.exp(top - highest), axis=1)
    loss = highest[:, 0] + jnp.log(summed) - jnp.sum(chosen, axis=1)
    columns = jnp.concatenate(
        [
            jnp.concatenate([loss, jnp.zeros((SECTIONS, 128 - CAP), F32)], axis=1),
            jnp.zeros((128 - SECTIONS, 128), F32),
        ],
        axis=0,
    ).T
    ids = ids_ref[...]
    owner = lax.broadcasted_iota(jnp.int32, (SECTIONS, tokens), 0)
    mine = jnp.where(ids == owner, 1.0, 0.0).astype(F32)
    earlier = lax.broadcasted_iota(jnp.int32, (tokens, tokens), 0)
    later = lax.broadcasted_iota(jnp.int32, (tokens, tokens), 1)
    upto = jnp.where(earlier <= later, 1.0, 0.0).astype(F32)
    within = jnp.dot(mine, upto, preferred_element_type=F32)
    slot = jnp.sum(within * mine, axis=0, keepdims=True)
    slot = (slot + 0.5).astype(jnp.int32) - 1
    place = lax.broadcasted_iota(jnp.int32, (CAP, tokens), 0)
    found = jnp.zeros((CAP, tokens), F32)
    for s in range(SECTIONS):
        found = jnp.where(ids == s, columns[0:CAP, s : s + 1], found)
    out_ref[...] = jnp.sum(jnp.where(place == slot, found, 0.0), axis=0, keepdims=True)


def combine(ids, stats):
    tokens = ids.shape[1]
    return pl.pallas_call(
        combine_kernel,
        out_shape=jax.ShapeDtypeStruct((1, tokens), F32),
        compiler_params=params(),
        cost_estimate=cost(2 * 8 * tokens * tokens, 400_000),
    )(ids, stats)


def split(blocks, width):
    held = jnp.concatenate(blocks, axis=0)
    wide = held[:, :width].astype(F32)
    high = lax.reduce_precision(wide, exponent_bits=8, mantissa_bits=7)
    both = jnp.concatenate([high, wide - high], axis=0).astype(BF16)
    return both, held[:, width:].astype(F32)


def relay(table, message, part):
    width = table.shape[1]
    return jnp.concatenate(
        [table, message[:, part : part + width], message[:, part + width :]], axis=0
    )


def body(hidden, cluster, label, proj, emb):
    x, z = lax.axis_index("x"), lax.axis_index("z")
    owner = lax.axis_index("y") * 2 + lax.axis_index("core")
    where = jnp.stack([owner, x, z]).astype(jnp.int32)
    ids = cluster.reshape(1, -1)
    weight, table = proj[0], emb[0]
    half = weight.shape[0] // 2
    wide = weight.shape[1]
    middle = table.shape[0] // 2

    deep = table.shape[0]
    right1, left1 = ring(weight, "z", Z, 1), ring(weight, "z", Z, -1)
    own_rows, up, down, words = select_rows(where, ids, label.reshape(1, -1), hidden)
    part = own_rows.shape[1]
    up, down = ring(up, "x", X, 1), ring(down, "x", X, -1)
    right1, left1, words = lax.optimization_barrier((right1, left1, words))
    right2, left2 = ring(right1, "z", Z, 1), ring(left1, "z", Z, -1)
    up, down, _, _ = lax.optimization_barrier((up, down, right1, left1))
    after = ring(relay(table, up, part), "x", X, 1)
    ahead = ring(relay(table, down, part), "x", X, -1)
    right3, left3 = ring(right2, "z", Z, 1), ring(left2, "z", Z, -1)
    front = ring(right3[:half], "z", Z, 1)
    back = ring(left3[half:], "z", Z, -1)
    front, back, after, ahead = lax.optimization_barrier((front, back, after, ahead))
    far1 = ring(after[:middle], "x", X, 1)
    far2 = ring(ahead[middle:deep], "x", X, -1)
    tables = [table, after, ahead, far1, far2]
    across = jnp.concatenate(
        [side[deep + i : deep + i + CAP] for side in (after, ahead) for i in (0, CAP)],
        axis=1,
    )
    rows = [own_rows, up, across, down]

    chunks = [weight, right1, left1, right2, left2, right3, left3]
    total = project_first(rows, chunks, [0, 7, 1, 6, 2, 5, 3])
    parts = project_last(total, rows, front, back, F32)
    own = parts[0]
    for k in (1, 3, 2):
        own = own + ring(parts[k].astype(F16), "x", X, -k).astype(F32)

    message = jnp.concatenate([own, words], axis=1).astype(F16)
    r1, l1 = ring(message, "z", Z, 1), ring(message, "z", Z, -1)
    r2, l2 = ring(message, "z", Z, 2), ring(message, "z", Z, -2)
    r3, l3 = ring(r2, "z", Z, 1), ring(l2, "z", Z, -1)
    edge = CAP // 2
    r4, l4 = ring(r2[:edge], "z", Z, 2), ring(l2[edge:], "z", Z, -2)

    stats = word_stats(where, *split([message, r1, l1, r2, l2], wide), tables)
    stats, r3, l3, r4, l4 = lax.optimization_barrier((stats, r3, l3, r4, l4))
    stats = word_stats(where, *split([r3, l3, r4, l4], wide), tables, stats)
    stats = stats.reshape(SECTIONS * Z, 2, 128)
    stats = lax.all_to_all(stats, ("y", "core", "z"), 0, 0, tiled=True)
    loss = combine(ids, stats.reshape(SECTIONS, Z, 2, 128))
    return loss.reshape(-1)


def solution(mesh):
    fine = Mesh(mesh.devices.reshape(4, 2, X, Z), ("y", "core", "x", "z"))
    return jax.shard_map(
        body,
        mesh=fine,
        in_specs=(
            P(("x", "z"), None),
            P(("x", "z"), None),
            P(("x", "z")),
            P(("y", "core"), ("x", "z"), None),
            P(("y", "core"), None, ("x", "z")),
        ),
        out_specs=P(("x", "z")),
        check_vma=False,
    )
```
